32 devices in a mesh: row: 4 (over y, x), col: 2 (over core), expert: 4 (over z).
Axes of the slice: x: 2, y: 2, z: 4, core: 2. Of those that a mesh axis runs over, the one named last changes fastest.
Arguments:
- tokens: bfloat16 [16384, 1024], P(('row', 'col', 'expert')), may hold values from -6 to 6
- query_weight: bfloat16 [1024, 1024], P('row', 'col'), may hold values from -0.75 to 0.75
- key_projection: bfloat16 [1024, 512], P('row', 'col'), may hold values from -0.75 to 0.75
- value_projection: bfloat16 [1024, 512], P('row', 'col'), may hold values from -0.1875 to 0.1875
- output_weight: bfloat16 [1024, 1024], P('row', 'col'), may hold values from -3 to 3
- router_weight: bfloat16 [1024, 32], P('row', 'col'), may hold values from -0.09375 to 0.09375
- attention_gain: bfloat16 [1024], P(('row', 'col')), may hold values from 0.5 to 1.5
- mixture_gain: bfloat16 [1024], P(('row', 'col')), may hold values from 0.5 to 1.5
- gate_weight: bfloat16 [1024, 32, 512], P(('row', 'col'), 'expert'), may hold values from -0.375 to 0.375
- up_weight: bfloat16 [1024, 32, 512], P(('row', 'col'), 'expert'), may hold values from -0.375 to 0.375
- down_weight: bfloat16 [1024, 32, 512], P(('row', 'col'), 'expert'), may hold values from -1 to 1
- choices: int32 [16384, 8], P(('row', 'col', 'expert')), may hold values from 0 to 31, all different within a row; in each aligned block of 512 rows (0 to 511, 512 to 1023, ...) at most 144 rows name the same one
- cotangent: bfloat16 [16384, 1024], P(('row', 'col', 'expert')), may hold values from -6 to 6
Outputs:
- layer_output: bfloat16 [16384, 1024], P(('row', 'col', 'expert'))
- input_gradient: float32 [16384, 1024], P(('row', 'col', 'expert'))
- query_gradient: float32 [1024, 1024], P('row', 'col')
- key_gradient: float32 [1024, 512], P('row', 'col')
- value_gradient: float32 [1024, 512], P('row', 'col')
- output_gradient: float32 [1024, 1024], P('row', 'col')
- router_gradient: float32 [1024, 32], P('row', 'col')
- attention_gradient: float32 [1024], P(('row', 'col'))
- mixture_gradient: float32 [1024], P(('row', 'col'))
- gate_gradient: float32 [1024, 32, 512], P(('row', 'col'), 'expert')
- up_gradient: float32 [1024, 32, 512], P(('row', 'col'), 'expert')
- down_gradient: float32 [1024, 32, 512], P(('row', 'col'), 'expert')
The draws below stay inside these ranges and needn't reach their ends.
Inputs may be any that keep to these rules, and one draw needn't show every extreme that they name: `choices`: in the rows of one device each token names 8 different experts, no expert is named by more than 144 rows, a bound that some block reaches.
All inputs are finite; a program needn't handle non-finite values.
Results may differ from the reference program's by a relative error of at most 0.02.
Values may be sent and summed in bfloat16 or wider, within the bound.
A program may use at most 256 MiB of HBM per device.

```python
import math
import jax
import jax.numpy as jnp
import numpy as np
from jax import lax

MODEL_WIDTH = 1024
QUERY_HEADS = 16
KEY_VALUE_HEADS = 8
HEAD_SIZE = 64
FF = 512
EXPERTS = 32
TOP = 8
TOK_DEV = 512
MOST = 144
TOKENS = 16384


def shard_levels(rng, extent, shards, low, high):
    level, own = 1.0, jax.random.fold_in(rng, 6)
    for dim, shards_of in shards:
        heights = jnp.exp(jax.random.uniform(jax.random.fold_in(own, dim), (shards_of,), jnp.float32, low / len(shards), high / len(shards)))
        level = level * jnp.repeat(heights, extent[dim] // shards_of).reshape([-1 if axis == dim else 1 for axis in range(len(extent))])
    return level


def assign_block(key, own, number, rows, number_of, top, bound, lean):
    ranking = jax.random.permutation(key, number_of)
    heavy_load, ordinary = load_shares(number_of, rows * top, bound, lean, True), load_shares(number_of, rows * top, bound, lean, False)
    places = jnp.arange(number_of)

    def named(lengths, offset_by):
        used = int((lengths > 0).sum())
        fixed = max(1, used // 4)
        passed = fixed + (places - fixed + offset_by * (used - fixed)) % max(1, number_of - fixed)
        return jnp.zeros((number_of,), jnp.int32).at[ranking[jnp.where(places < fixed, places, passed)]].set(jnp.asarray(lengths, jnp.int32))

    lengths = jnp.where(number % 4 == 0, named(heavy_load, number // 4), named(ordinary, number - number // 4 - 1))
    mixed = jax.random.permutation(jax.random.fold_in(own, 3), number_of)
    source_of, receiver = mixed[0:number_of // 2 * 2:2], mixed[1:number_of // 2 * 2:2]
    slack = jnp.minimum(lengths[source_of] - 1, bound - lengths[receiver]) // 2
    slack = jnp.where((source_of == ranking[0]) | (receiver == ranking[0]) | (lengths[receiver] == 0), 0, jnp.maximum(slack, 0))
    passed = jax.random.randint(jax.random.fold_in(own, 4), (number_of // 2,), 0, 1 << 20) % (slack + 1)
    lengths = lengths.at[source_of].add(-passed).at[receiver].add(passed)
    items = jnp.searchsorted(jnp.cumsum(lengths), jnp.arange(rows * top), side="right").astype(jnp.int32)
    listing = items.reshape(top, rows).T
    listing = listing[jax.random.permutation(jax.random.fold_in(own, 1), rows)]
    offset_by = jax.random.randint(jax.random.fold_in(own, 2), (rows, 1), 0, top)
    return jnp.take_along_axis(listing, (jnp.arange(top)[None, :] + offset_by) % top, axis=1)


def load_shares(number_of, total, most, skew, full):
    loads = [(1 << 20) // math.isqrt(grade ** skew) + 1 for grade in range(1, number_of + 1)]
    largest = most if full else min(most, max(-(-total // number_of), total * loads[0] // sum(loads)))
    least = 1 if total - largest >= number_of - 1 else 0
    counts, rest = [largest] + [least] * (number_of - 1), total - largest - least * (number_of - 1)
    while rest > 0:
        candidates = [i for i in range(1, number_of) if counts[i] < largest] or [i for i in range(1, number_of) if counts[i] < most]
        mass, left = sum([loads[i] for i in candidates]), rest
        for i in candidates:
            addition = min(most - counts[i], max(1, left * loads[i] // mass), rest)
            counts[i] = counts[i] + addition
            rest = rest - addition
    return np.array(counts)


def centred(stream_key, dims, width, reach, split=(), held_as=jnp.bfloat16):
    level = shard_levels(stream_key, dims, split, -0.22, 0.18) if split else 1.0
    values = jax.random.normal(stream_key, dims, jnp.float32) * width * level
    return jnp.minimum(jnp.maximum(values, -reach), reach).astype(held_as)


def setup_inputs(seed: int = 0) -> dict:
    streams_of = jax.random.split(jax.random.key(seed), 14)
    tokens = centred(streams_of[0], (TOKENS, MODEL_WIDTH), 1.0, 6.0, ((0, 32),))
    query_weight = centred(streams_of[1], (MODEL_WIDTH, QUERY_HEADS * HEAD_SIZE), (MODEL_WIDTH // 16) ** -0.5, 0.75, ((0, 4), (1, 2)))
    key_projection = centred(streams_of[2], (MODEL_WIDTH, KEY_VALUE_HEADS * HEAD_SIZE), (MODEL_WIDTH // 16) ** -0.5, 0.75, ((0, 4), (1, 2)))
    value_projection = centred(streams_of[3], (MODEL_WIDTH, KEY_VALUE_HEADS * HEAD_SIZE), MODEL_WIDTH ** -0.5, 0.1875, ((0, 4), (1, 2)))
    output_weight = centred(streams_of[4], (QUERY_HEADS * HEAD_SIZE, MODEL_WIDTH), (max(QUERY_HEADS * HEAD_SIZE // 256, 1)) ** -0.5, 3.0, ((0, 4), (1, 2)))
    router_weight = centred(streams_of[5], (MODEL_WIDTH, EXPERTS), (4 * MODEL_WIDTH) ** -0.5, 0.09375, ((0, 4), (1, 2)))
    attention_gain = jnp.clip(1.0 + 0.1 * jax.random.normal(streams_of[6], (MODEL_WIDTH,), jnp.float32), 0.5, 1.5).astype(jnp.bfloat16)
    mixture_gain = jnp.clip(1.0 + 0.1 * jax.random.normal(streams_of[7], (MODEL_WIDTH,), jnp.float32), 0.5, 1.5).astype(jnp.bfloat16)
    gate_weight = centred(streams_of[8], (MODEL_WIDTH, EXPERTS, FF), (MODEL_WIDTH // 4) ** -0.5, 0.375, ((0, 8), (1, 4)))
    up_weight = centred(streams_of[9], (MODEL_WIDTH, EXPERTS, FF), (MODEL_WIDTH // 4) ** -0.5, 0.375, ((0, 8), (1, 4)))
    down_weight = centred(streams_of[10], (MODEL_WIDTH, EXPERTS, FF), (FF // 16) ** -0.5, 1.0, ((0, 8), (1, 4)))
    choices_keys = jax.random.split(jax.random.fold_in(streams_of[11], 1), TOKENS // TOK_DEV)
    choices_turns = jax.random.permutation(jax.random.fold_in(streams_of[11], 3), TOKENS // TOK_DEV)
    choices = jax.vmap(lambda own, number: assign_block(jax.random.fold_in(streams_of[11], 2), own, number, TOK_DEV, EXPERTS, TOP, MOST, 1))(choices_keys, choices_turns).reshape((TOKENS, TOP))
    cotangent = centred(streams_of[12], (TOKENS, MODEL_WIDTH), 1.0, 6.0, ((0, 32),))
    return dict(tokens=tokens, query_weight=query_weight, key_projection=key_projection, value_projection=value_projection, output_weight=output_weight, router_weight=router_weight, attention_gain=attention_gain, mixture_gain=mixture_gain, gate_weight=gate_weight, up_weight=up_weight, down_weight=down_weight, choices=choices, cotangent=cotangent)


@jax.custom_vjp
def lower_half(v):
    return lax.optimization_barrier(v.astype(jnp.bfloat16)).astype(jnp.float32)

@jax.custom_vjp
def low_back(v):
    return v

def low_keep(v):
    return (lower_half(v), None)

def low_pass(kept, grad):
    return (grad,)

def back_keep(v):
    return (v, None)

def back_low(kept, grad):
    return (lower_half(grad),)
lower_half.defvjp(low_keep, low_pass)
low_back.defvjp(back_keep, back_low)
score_factor = 0.015625
branch_factor = 0.22
norm_epsilon = 1e-06
rotary_base = 10000.0
masked_score = -1e+30

def product(left, right):
    return jnp.dot(left, right, precision=lax.Precision.HIGHEST)

def root_norm(values, gain_row):
    return values * lax.rsqrt(lax.optimization_barrier(jnp.mean(values * values, axis=-1, keepdims=True)) + norm_epsilon) * gain_row

def rotary_tables(sequence_length):
    half_width = HEAD_SIZE // 2
    inverse = rotary_base ** (-(jnp.arange(half_width, dtype=jnp.float32) * 2.0 / HEAD_SIZE))
    angles = jnp.arange(sequence_length, dtype=jnp.float32)[:, None] * inverse[None, :]
    cosine_values = jnp.concatenate([jnp.cos(angles), jnp.cos(angles)], axis=1)
    sine_values = jnp.concatenate([jnp.sin(angles), jnp.sin(angles)], axis=1)
    return (cosine_values, sine_values)

def apply_rotation(values, cosine_values, sine_values):
    half_width = values.shape[-1] // 2
    turned = jnp.concatenate([-values[..., half_width:], values[..., :half_width]], axis=-1)
    return values * cosine_values + turned * sine_values

def slot_tables(choice_rows):
    flat_ids = choice_rows.reshape(-1)
    count_all = flat_ids.shape[0]
    one_hot = (flat_ids[:, None] == jnp.arange(EXPERTS, dtype=jnp.int32)[None, :]).astype(jnp.int32)
    earlier = jnp.cumsum(one_hot, axis=0) - one_hot
    slot_rank = lax.optimization_barrier(jnp.sum(earlier * one_hot, axis=1))
    slot_index = (flat_ids * MOST + slot_rank).astype(jnp.int32)
    assign_of = jnp.zeros((EXPERTS * MOST,), jnp.int32).at[slot_index].set(jnp.arange(count_all, dtype=jnp.int32))
    filled = jnp.zeros((EXPERTS * MOST,), jnp.int32).at[slot_index].set(1)
    return (slot_index, assign_of, filled)

def layer(inputs, query_weight, key_projection, value_projection, output_weight, router_weight, attention_gain, mixture_gain, gate_weight, up_weight, down_weight, choice_rows, slot_index, assign_of, filled):
    sequence_length = inputs.shape[0]
    query_groups = QUERY_HEADS // KEY_VALUE_HEADS
    cosine_values, sine_values = rotary_tables(sequence_length)
    normed = lower_half(root_norm(inputs, attention_gain))
    query_matrix = low_back(product(normed, query_weight))
    key_matrix = low_back(product(normed, key_projection))
    value_matrix = lower_half(low_back(product(normed, value_projection)))
    query_rotated = lower_half(apply_rotation(query_matrix.reshape(sequence_length, KEY_VALUE_HEADS, query_groups, HEAD_SIZE).transpose(1, 2, 0, 3), cosine_values, sine_values))
    key_rotated = lower_half(apply_rotation(key_matrix.reshape(sequence_length, KEY_VALUE_HEADS, HEAD_SIZE).transpose(1, 0, 2), cosine_values, sine_values))
    value_head_rows = value_matrix.reshape(sequence_length, KEY_VALUE_HEADS, HEAD_SIZE).transpose(1, 0, 2)
    scores = jnp.einsum('hgqd,hkd->hgqk', query_rotated, key_rotated, precision=lax.Precision.HIGHEST) * score_factor
    causal = jnp.arange(sequence_length)[:, None] >= jnp.arange(sequence_length)[None, :]
    scores = low_back(jnp.where(causal, scores, masked_score))
    weights_low = lower_half(jax.nn.softmax(scores, axis=-1))
    mixed_heads = jnp.einsum('hgqk,hkd->hgqd', weights_low, value_head_rows, precision=lax.Precision.HIGHEST)
    mixed_low = lower_half(low_back(mixed_heads.transpose(2, 0, 1, 3).reshape(sequence_length, QUERY_HEADS * HEAD_SIZE)))
    branch = low_back(product(mixed_low, output_weight))
    middle = inputs + branch_factor * branch
    second = lower_half(root_norm(middle, mixture_gain))
    logits = low_back(product(second, router_weight))
    chosen = jnp.take_along_axis(logits, choice_rows, axis=1)
    router_gates = jax.nn.softmax(chosen, axis=1)
    live = (filled > 0)[:, None]
    rows_in = low_back(jnp.where(live, second[assign_of // TOP], 0.0)).reshape(EXPERTS, MOST, MODEL_WIDTH)
    gate_pre = low_back(jnp.einsum('ecd,def->ecf', rows_in, gate_weight, precision=lax.Precision.HIGHEST))
    up_pre = low_back(jnp.einsum('ecd,def->ecf', rows_in, up_weight, precision=lax.Precision.HIGHEST))
    activated = lower_half(jax.nn.silu(gate_pre) * up_pre)
    expert_out = lower_half(low_back(jnp.einsum('ecf,def->ecd', activated, down_weight, precision=lax.Precision.HIGHEST)))
    picked_rows = expert_out.reshape(EXPERTS * MOST, MODEL_WIDTH)[slot_index].reshape(sequence_length, TOP, MODEL_WIDTH)
    combined = lax.optimization_barrier(jnp.sum(router_gates[:, :, None] * picked_rows, axis=1))
    return middle + branch_factor * combined

def reference(tokens, query_weight, key_projection, value_projection, output_weight, router_weight, attention_gain, mixture_gain, gate_weight, up_weight, down_weight, choices, cotangent):
    weights = tuple((array_item.astype(jnp.float32) for array_item in (query_weight, key_projection, value_projection, output_weight, router_weight, attention_gain, mixture_gain, gate_weight, up_weight, down_weight)))
    block_count = TOKENS // TOK_DEV
    token_blocks = tokens.reshape(block_count, TOK_DEV, MODEL_WIDTH)
    choice_blocks = choices.reshape(block_count, TOK_DEV, TOP)
    cotangent_blocks = cotangent.reshape(block_count, TOK_DEV, MODEL_WIDTH)

    def one_block(totals, block_data):
        token_rows, choice_rows, cotangent_rows = block_data
        slot_index, assign_of, filled = slot_tables(choice_rows)

        def forward(inputs, *params):
            return layer(inputs, *params, choice_rows, slot_index, assign_of, filled)
        result, pull_back = jax.vjp(forward, token_rows.astype(jnp.float32), *weights)
        pulled = pull_back(cotangent_rows.astype(jnp.float32))
        totals = tuple((running + gradient for running, gradient in zip(totals, pulled[1:])))
        return (totals, (result.astype(jnp.bfloat16), pulled[0]))
    zero_totals = tuple((jnp.zeros(array_item.shape, jnp.float32) for array_item in weights))
    totals, (outputs, input_grads) = lax.scan(one_block, zero_totals, (token_blocks, choice_blocks, cotangent_blocks))
    return (outputs.reshape(TOKENS, MODEL_WIDTH), input_grads.reshape(TOKENS, MODEL_WIDTH), totals[0], totals[1], totals[2], totals[3], totals[4], totals[5], totals[6], totals[7], totals[8], totals[9])
```

```python
import functools

import jax
import jax.numpy as jnp
from jax import lax
from jax.experimental import pallas as pl
from jax.experimental.pallas import tpu as pltpu
from jax.sharding import PartitionSpec as P

HEAD_SIZE = 64
EXPERTS = 32
MOST = 144

score_factor = 0.015625
branch_factor = 0.22
norm_epsilon = 1e-06
rotary_base = 10000.0
masked_score = -1e30
bf16 = jnp.bfloat16
f32 = jnp.float32


def dot(a, b, a_dim, b_dim):
    return lax.dot_general(a, b, (((a_dim,), (b_dim,)), ((), ())), preferred_element_type=f32)


def rotary_tables(sequence_length):
    half_width = HEAD_SIZE // 2
    inverse = rotary_base ** (-(jnp.arange(half_width, dtype=f32) * 2.0 / HEAD_SIZE))
    angles = jnp.arange(sequence_length, dtype=f32)[:, None] * inverse[None, :]
    cosine, sine = jnp.cos(angles), jnp.sin(angles)
    return (
        jnp.concatenate([cosine] * 4, axis=1),
        jnp.concatenate([-sine, sine, -sine, sine], axis=1),
    )


def turned(values):
    half = HEAD_SIZE // 2
    lane = lax.broadcasted_iota(jnp.int32, values.shape, 1)
    ahead = pltpu.roll(values, values.shape[1] - half, 1)
    behind = pltpu.roll(values, half, 1)
    return jnp.where(lane % HEAD_SIZE < half, ahead, behind)


def causal_scores(query, keys, begin):
    scores = dot(query, keys, 1, 1) * score_factor
    rows = begin + lax.broadcasted_iota(jnp.int32, scores.shape, 0)
    return jnp.where(rows >= lax.broadcasted_iota(jnp.int32, scores.shape, 1), scores, masked_score)


def attention_forward(
    query_width, key_width, qkv_ref, cos_ref, sin_ref, query_ref, key_ref, value_ref, mixed_ref, log_ref
):
    length = qkv_ref.shape[1]
    block = min(256, length)
    cosine, sine = cos_ref[...], sin_ref[...]
    for start in range(0, query_width + key_width, 128):
        values = qkv_ref[0, :, start : start + 128]
        rotated = (values * cosine + turned(values) * sine).astype(bf16)
        if start < query_width:
            query_ref[0, :, start : start + 128] = rotated
        else:
            key_ref[0, :, start - query_width : start - query_width + 128] = rotated
    value_ref[0] = qkv_ref[0, :, query_width + key_width :].astype(bf16)
    groups = query_width // key_width
    lane = lax.broadcasted_iota(jnp.int32, (block, 128), 1)
    for begin in range(0, length, block):
        end = begin + block
        logs = jnp.zeros((block, 128), f32)
        for head in range(query_width // HEAD_SIZE):
            here = slice(head * HEAD_SIZE, (head + 1) * HEAD_SIZE)
            shared = slice(head // groups * HEAD_SIZE, (head // groups + 1) * HEAD_SIZE)
            scores = causal_scores(query_ref[0, begin:end, here], key_ref[0, :end, shared], begin)
            row_max = jnp.max(scores, axis=1, keepdims=True)
            weights = jnp.exp(scores - row_max)
            total = jnp.sum(weights, axis=1, keepdims=True)
            probs = (weights * (1.0 / total)).astype(bf16)
            mixed_ref[begin:end, here] = dot(probs, value_ref[0, :end, shared], 1, 0).astype(bf16)
            logs = jnp.where(lane == head, row_max + jnp.log(total), logs)
        log_ref[0, begin:end, :] = logs


def attention_backward(
    query_width,
    key_width,
    query_ref,
    key_ref,
    value_ref,
    grad_ref,
    log_ref,
    cos_ref,
    sin_ref,
    out_ref,
    dq_ref,
    dk_ref,
    dv_ref,
):
    length = query_ref.shape[1]
    block = min(256, length)
    groups = query_width // key_width
    dk_ref[...] = jnp.zeros_like(dk_ref)
    dv_ref[...] = jnp.zeros_like(dv_ref)
    for begin in range(0, length, block):
        end = begin + block
        for head in range(query_width // HEAD_SIZE):
            here = slice(head * HEAD_SIZE, (head + 1) * HEAD_SIZE)
            shared = slice(head // groups * HEAD_SIZE, (head // groups + 1) * HEAD_SIZE)
            query = query_ref[0, begin:end, here]
            keys = key_ref[0, :end, shared]
            grads = grad_ref[begin:end, here]
            scores = causal_scores(query, keys, begin)
            weights = jnp.exp(scores - log_ref[0, begin:end, head : head + 1])
            weight_grad = dot(grads, value_ref[0, :end, shared], 1, 1)
            spread = jnp.sum(weights * weight_grad, axis=1, keepdims=True)
            score_grad = (weights * (weight_grad - spread)).astype(bf16)
            dq_ref[begin:end, here] = dot(score_grad, keys, 1, 0) * score_factor
            dk_ref[:end, shared] += dot(score_grad, query, 0, 0) * score_factor
            dv_ref[:end, shared] += dot(weights.astype(bf16), grads, 0, 0)
    cosine, sine = cos_ref[...], sin_ref[...]
    for start in range(0, query_width + key_width, 128):
        if start < query_width:
            values = dq_ref[:, start : start + 128]
        else:
            values = dk_ref[:, start - query_width : start - query_width + 128]
        out_ref[0, :, start : start + 128] = (values * cosine - turned(values) * sine).astype(bf16)
    out_ref[0, :, query_width + key_width :] = dv_ref[...].astype(bf16)


def params(count):
    return pltpu.CompilerParams(
        dimension_semantics=("arbitrary",) * count, vmem_limit_bytes=56 * 1024 * 1024
    )


def run_forward(qkv, cosine, sine, query_width, key_width):
    parts, length, width = qkv.shape
    whole = lambda c: (c, 0, 0)
    table = pl.BlockSpec((length, 128), lambda c: (0, 0))
    return pl.pallas_call(
        functools.partial(attention_forward, query_width, key_width),
        grid=(parts,),
        in_specs=[pl.BlockSpec((1, length, width), whole), table, table],
        out_specs=[
            pl.BlockSpec((1, length, query_width), whole),
            pl.BlockSpec((1, length, key_width), whole),
            pl.BlockSpec((1, length, key_width), whole),
            pl.BlockSpec((length, query_width), lambda c: (0, c)),
            pl.BlockSpec((1, length, 128), whole),
        ],
        out_shape=[
            jax.ShapeDtypeStruct((parts, length, query_width), bf16),
            jax.ShapeDtypeStruct((parts, length, key_width), bf16),
            jax.ShapeDtypeStruct((parts, length, key_width), bf16),
            jax.ShapeDtypeStruct((length, parts * query_width), bf16),
            jax.ShapeDtypeStruct((parts, length, 128), f32),
        ],
        compiler_params=params(1),
        cost_estimate=pl.CostEstimate(
            flops=4 * length * length * parts * query_width,
            bytes_accessed=8 * parts * length * width,
            transcendentals=parts * length * length * query_width // HEAD_SIZE,
        ),
        name="attention_forward",
    )(qkv, cosine, sine)


def run_backward(query, key, value, grad, logs, cosine, sine):
    parts, length, query_width = query.shape
    key_width = key.shape[2]
    width = query_width + 2 * key_width
    whole = lambda c: (c, 0, 0)
    table = pl.BlockSpec((length, 128), lambda c: (0, 0))
    return pl.pallas_call(
        functools.partial(attention_backward, query_width, key_width),
        grid=(parts,),
        in_specs=[
            pl.BlockSpec((1, length, query_width), whole),
            pl.BlockSpec((1, length, key_width), whole),
            pl.BlockSpec((1, length, key_width), whole),
            pl.BlockSpec((length, query_width), lambda c: (0, c)),
            pl.BlockSpec((1, length, 128), whole),
            table,
            table,
        ],
        out_specs=pl.BlockSpec((1, length, width), whole),
        out_shape=jax.ShapeDtypeStruct((parts, length, width), bf16),
        scratch_shapes=[
            pltpu.VMEM((length, query_width), f32),
            pltpu.VMEM((length, key_width), f32),
            pltpu.VMEM((length, key_width), f32),
        ],
        compiler_params=params(1),
        cost_estimate=pl.CostEstimate(
            flops=10 * length * length * parts * query_width,
            bytes_accessed=6 * parts * length * width,
            transcendentals=parts * length * length * query_width // HEAD_SIZE,
        ),
        name="attention_backward",
    )(query, key, value, grad, logs, cosine, sine)


def dispatch_kernel(slot_ref, gate_ref, second_ref, grad_ref, rows_ref, grads_ref, gates_ref):
    expert = pl.program_id(1)
    slots = slot_ref[0, pl.ds(expert, 1), :]
    gates = gate_ref[0, pl.ds(expert, 1), :]
    match = lax.broadcasted_iota(jnp.int32, (MOST, slots.shape[1]), 0) == slots
    picks = match.astype(f32).astype(bf16)
    rows_ref[0, 0] = dot(picks, second_ref[0], 1, 0).astype(bf16)
    grads_ref[0, 0] = dot(picks, grad_ref[0], 1, 0).astype(bf16)
    gate_column = jnp.sum(jnp.where(match, gates, 0.0), axis=1, keepdims=True)
    gates_ref[0, 0] = jnp.broadcast_to(gate_column, (MOST, 128))


def run_dispatch(slots, gates, second, grad):
    sources, experts, length = slots.shape
    width = second.shape[2]
    table = pl.BlockSpec((1, experts, length), lambda s, e: (s, 0, 0))
    rows = pl.BlockSpec((1, length, width), lambda s, e: (s, 0, 0))
    out = lambda n: pl.BlockSpec((1, 1, MOST, n), lambda s, e: (e, s, 0, 0))
    return pl.pallas_call(
        dispatch_kernel,
        grid=(sources, experts),
        in_specs=[table, table, rows, rows],
        out_specs=[out(width), out(width), out(128)],
        out_shape=[
            jax.ShapeDtypeStruct((experts, sources, MOST, width), bf16),
            jax.ShapeDtypeStruct((experts, sources, MOST, width), bf16),
            jax.ShapeDtypeStruct((experts, sources, MOST, 128), f32),
        ],
        compiler_params=params(2),
        cost_estimate=pl.CostEstimate(
            flops=4 * sources * experts * MOST * length * width,
            bytes_accessed=4 * sources * experts * MOST * width,
            transcendentals=0,
        ),
        name="dispatch",
    )(slots, gates, second, grad)


def expert_kernel(rows_ref, grads_ref, gates_ref, weight_ref, out_ref, back_ref, gate_grad_ref, weight_grad_ref):
    sources, slots, width = rows_ref.shape[1:]
    count = sources * slots
    pieces, _, _, part, hidden = weight_ref.shape
    rows = rows_ref[0].reshape(count, width)
    grads = grads_ref[0].reshape(count, width)
    gates = gates_ref[0].reshape(count, 128)[:, :1] * branch_factor
    gate_weight = weight_ref[:, 0, 0].reshape(width, hidden)
    up_weight = weight_ref[:, 1, 0].reshape(width, hidden)
    down_weight = weight_ref[:, 2, 0].reshape(width, hidden)
    gate_pre = dot(rows, gate_weight, 1, 0)
    up_pre = dot(rows, up_weight, 1, 0)
    sigmoid = 1.0 / (1.0 + jnp.exp(-gate_pre))
    silu = gate_pre * sigmoid
    act = (silu * up_pre).astype(bf16).astype(f32)
    act_raw = dot(grads, down_weight, 1, 0)
    gate_grad = jnp.sum(act * act_raw, axis=1, keepdims=True) * branch_factor
    gate_grad_ref[0] = jnp.broadcast_to(gate_grad, (count, 128)).reshape(sources, slots, 128)
    scaled = (gates * act).astype(bf16)
    act_grad = gates * act_raw
    gate_low = (act_grad * up_pre * sigmoid * (1.0 + gate_pre * (1.0 - sigmoid))).astype(bf16)
    up_low = (act_grad * silu).astype(bf16)
    back = dot(gate_low, gate_weight, 1, 1) + dot(up_low, up_weight, 1, 1)
    back_ref[0] = back.astype(bf16).reshape(sources, slots, width)
    out_ref[0] = dot(scaled, down_weight, 1, 1).astype(bf16).reshape(sources, slots, width)
    shape = (pieces, part, hidden)
    weight_grad_ref[:, 0, 0] = dot(rows, gate_low, 0, 0).astype(bf16).reshape(shape)
    weight_grad_ref[:, 1, 0] = dot(rows, up_low, 0, 0).astype(bf16).reshape(shape)
    weight_grad_ref[:, 2, 0] = dot(grads, scaled, 0, 0).astype(bf16).reshape(shape)


def run_experts(rows, grads, gates, weights):
    experts, sources, slots, width = rows.shape
    pieces, kinds, _, part, hidden = weights.shape
    row = lambda n: pl.BlockSpec((1, sources, slots, n), lambda e: (e, 0, 0, 0))
    weight = pl.BlockSpec((pieces, kinds, 1, part, hidden), lambda e: (0, 0, e, 0, 0))
    return pl.pallas_call(
        expert_kernel,
        grid=(experts,),
        in_specs=[row(width), row(width), row(128), weight],
        out_specs=[row(width), row(width), row(128), weight],
        out_shape=[
            jax.ShapeDtypeStruct(rows.shape, bf16),
            jax.ShapeDtypeStruct(rows.shape, bf16),
            jax.ShapeDtypeStruct(gates.shape, f32),
            jax.ShapeDtypeStruct(weights.shape, bf16),
        ],
        compiler_params=params(1),
        cost_estimate=pl.CostEstimate(
            flops=18 * experts * sources * slots * width * hidden,
            bytes_accessed=8 * experts * sources * slots * width + 4 * weights.size,
            transcendentals=experts * sources * slots * hidden,
        ),
        name="experts",
    )(rows, grads, gates, weights)


def combine_kernel(slot_ref, rows_ref, out_ref, picks_ref):
    experts, length = slot_ref.shape[1:]
    for expert in range(experts):
        match = lax.broadcasted_iota(jnp.int32, (MOST, length), 0) == slot_ref[0, expert : expert + 1, :]
        picks_ref[expert * MOST : (expert + 1) * MOST, :] = match.astype(f32).astype(bf16)
    rows = rows_ref[:, 0].reshape(experts * MOST, rows_ref.shape[3])
    out_ref[0] = dot(picks_ref[...], rows, 0, 0).astype(bf16)


def combine_gates_kernel(slot_ref, rows_ref, gate_ref, out_ref, gate_out_ref, picks_ref):
    combine_kernel(slot_ref, rows_ref, out_ref, picks_ref)
    experts, length = slot_ref.shape[1:]
    for expert in range(experts):
        match = lax.broadcasted_iota(jnp.int32, (MOST, length), 0) == slot_ref[0, expert : expert + 1, :]
        column = gate_ref[expert, 0][:, :1]
        gate_out_ref[0, expert : expert + 1, :] = jnp.sum(
            jnp.where(match, column, 0.0), axis=0, keepdims=True
        )


def run_combine(slots, rows, gate_grads=None):
    sources, experts, length = slots.shape
    width = rows.shape[3]
    table = pl.BlockSpec((1, experts, length), lambda s: (s, 0, 0))
    row = lambda n: pl.BlockSpec((experts, 1, MOST, n), lambda s: (0, s, 0, 0))
    out_spec = pl.BlockSpec((1, length, width), lambda s: (s, 0, 0))
    out_shape = jax.ShapeDtypeStruct((sources, length, width), bf16)
    common = dict(
        grid=(sources,),
        scratch_shapes=[pltpu.VMEM((experts * MOST, length), bf16)],
        compiler_params=params(1),
        cost_estimate=pl.CostEstimate(
            flops=2 * sources * experts * MOST * length * width,
            bytes_accessed=2 * rows.size + 2 * sources * length * width,
            transcendentals=0,
        ),
    )
    if gate_grads is None:
        return pl.pallas_call(
            combine_kernel,
            in_specs=[table, row(width)],
            out_specs=out_spec,
            out_shape=out_shape,
            name="combine",
            **common,
        )(slots, rows)
    return pl.pallas_call(
        combine_gates_kernel,
        in_specs=[table, row(width), row(128)],
        out_specs=[out_spec, table],
        out_shape=[out_shape, jax.ShapeDtypeStruct(slots.shape, f32)],
        name="combine_gates",
        **common,
    )(slots, rows, gate_grads)


def inverse_norm(values):
    return lax.rsqrt(jnp.mean(values * values, axis=-1, keepdims=True) + norm_epsilon)


def norm_back(incoming, values, inverse, gain_row):
    scaled = incoming * gain_row
    mean = jnp.mean(scaled * values, axis=-1, keepdims=True)
    grad = inverse * scaled - values * (inverse * inverse * inverse * mean)
    return grad, jnp.sum(incoming * values * inverse, axis=0)


def join_parts(parts, joined, cuts):
    if joined == 1:
        return parts
    count, width, _ = parts.shape
    pieces = jnp.split(parts, cuts, axis=2)
    return jnp.concatenate(
        [
            piece.reshape(count // joined, joined, width, -1)
            .transpose(0, 2, 1, 3)
            .reshape(count // joined, width, -1)
            for piece in pieces
        ],
        axis=2,
    )


def split_parts(parts, joined, cuts):
    if joined == 1:
        return parts
    count, width, _ = parts.shape
    pieces = jnp.split(parts, [cut * joined for cut in cuts], axis=2)
    return jnp.concatenate(
        [
            piece.reshape(count, width, joined, -1)
            .transpose(0, 2, 1, 3)
            .reshape(count * joined, width, -1)
            for piece in pieces
        ],
        axis=2,
    )


def shards(
    tokens,
    query_weight,
    key_projection,
    value_projection,
    output_weight,
    router_weight,
    attention_gain,
    mixture_gain,
    gate_weight,
    up_weight,
    down_weight,
    choices,
    cotangent,
):
    col_count, row_count, sources = (lax.axis_size(name) for name in ("col", "row", "expert"))
    length, width = tokens.shape
    query_width, key_width, output_width = (
        query_weight.shape[1],
        key_projection.shape[1],
        output_weight.shape[1],
    )
    router_width = router_weight.shape[1]
    local_experts = gate_weight.shape[1]
    inner = query_width + 2 * key_width

    gains = lax.all_gather(jnp.stack([attention_gain, mixture_gain]), ("row", "col"), axis=1, tiled=True)
    packed = jnp.concatenate(
        [query_weight, key_projection, value_projection, output_weight, router_weight], axis=1
    )
    packed = lax.all_gather(packed, ("col", "row"), axis=0, tiled=True)
    packed = packed.reshape(col_count, width, packed.shape[1])
    joined = max(1, 128 // key_width)
    cuts = (query_width, query_width + key_width)
    inner_weight = join_parts(packed[:, :, :inner], joined, cuts)
    outer_weight = packed[:, :, inner : inner + output_width]
    router_parts = packed[:, :, inner + output_width :]
    router_full = router_parts.transpose(1, 0, 2).reshape(width, EXPERTS)

    choices_all = lax.all_gather(choices, "expert", axis=0)
    cotangent_all = lax.all_gather(cotangent, "expert", axis=0)
    weights = jnp.stack([gate_weight, up_weight, down_weight]).transpose(0, 2, 1, 3)
    weights_all = lax.all_gather(weights, ("row", "col"), axis=0)

    expert_ids = jnp.arange(EXPERTS, dtype=jnp.int32)
    chosen = jnp.any(
        choices_all.transpose(0, 2, 1)[:, :, None, :] == expert_ids[None, None, :, None], axis=1
    )
    earlier = (jnp.arange(length)[:, None] < jnp.arange(length)[None, :]).astype(bf16)
    ranks = jnp.einsum("set,tu->seu", chosen.astype(bf16), earlier, preferred_element_type=f32)
    slots_all = jnp.where(chosen, ranks.astype(jnp.int32), -1)
    source = lax.axis_index("expert")
    slots = lax.dynamic_slice_in_dim(slots_all, source * local_experts, local_experts, axis=1)

    cosine, sine = rotary_tables(length)
    attention_full, mixture_full = gains[0].astype(f32), gains[1].astype(f32)
    inputs = tokens.astype(f32)
    first_inverse = inverse_norm(inputs)
    normed = (attention_full * inputs * first_inverse).astype(bf16)
    qkv = jnp.einsum("td,cdf->ctf", normed, inner_weight, preferred_element_type=f32)
    query_rot, key_rot, value_low, mixed, logs = run_forward(
        qkv, cosine, sine, query_width * joined, key_width * joined
    )
    branch = jnp.concatenate(
        [jnp.dot(mixed, outer_weight[c], preferred_element_type=f32) for c in range(col_count)], axis=1
    )
    middle = inputs + branch_factor * branch
    second_inverse = inverse_norm(middle)
    second = (mixture_full * middle * second_inverse).astype(bf16)

    second_all = lax.all_gather(second, "expert", axis=0)
    logits = jnp.einsum("de,std->set", router_full, second_all, preferred_element_type=f32)
    top = jnp.max(jnp.where(chosen, logits, masked_score), axis=1, keepdims=True)
    exped = jnp.where(chosen, jnp.exp(jnp.where(chosen, logits - top, 0.0)), 0.0)
    gates_all = exped / jnp.sum(exped, axis=1, keepdims=True)
    gates = lax.dynamic_slice_in_dim(gates_all, source * local_experts, local_experts, axis=1)
    own_gates = lax.dynamic_index_in_dim(gates_all, source, axis=0, keepdims=False)

    rows, grads, slot_gates = run_dispatch(slots, gates, second_all, cotangent_all)
    outs, backs, slot_gate_grads, weight_grads = run_experts(rows, grads, slot_gates, weights_all)
    back_sums, gate_grads = run_combine(slots, backs, slot_gate_grads)
    gate_grads = lax.all_to_all(gate_grads, "expert", split_axis=0, concat_axis=0).reshape(EXPERTS, length)
    second_grad = lax.psum_scatter(back_sums, "expert", scatter_dimension=0).astype(f32)
    out_sums = run_combine(slots, outs)
    combined = lax.psum_scatter(out_sums, "expert", scatter_dimension=0).astype(f32)
    layer_output = (middle + combined).astype(bf16)
    expert_sums = lax.psum_scatter(weight_grads, ("row", "col"), scatter_dimension=0)
    expert_sums = expert_sums.transpose(0, 2, 1, 3).astype(f32)

    mean_grad = jnp.sum(own_gates * gate_grads, axis=0, keepdims=True)
    logit_grad = (own_gates * (gate_grads - mean_grad)).astype(bf16)
    router_part = jnp.einsum("td,et->de", second, logit_grad, preferred_element_type=f32)
    second_grad = second_grad + jnp.einsum(
        "et,de->td", logit_grad, router_full, preferred_element_type=f32
    )
    middle_norm_grad, mixture_part = norm_back(second_grad, middle, second_inverse, mixture_full)
    middle_grad = cotangent.astype(f32) + middle_norm_grad
    branch_grad = (branch_factor * middle_grad).astype(bf16)
    branch_parts = [
        branch_grad[:, c * output_width : (c + 1) * output_width] for c in range(col_count)
    ]
    mixed_grad = sum(
        jnp.einsum("td,fd->tf", branch_parts[c], outer_weight[c], preferred_element_type=f32)
        for c in range(col_count)
    ).astype(bf16)
    output_parts = jnp.stack(
        [
            jnp.concatenate(
                [
                    jnp.einsum("tf,td->fd", mixed, branch_parts[c], preferred_element_type=f32),
                    router_part[:, c * router_width : (c + 1) * router_width],
                ],
                axis=1,
            ).astype(bf16)
            for c in range(col_count)
        ]
    )
    outer_sums = lax.psum_scatter(
        output_parts.reshape(col_count * width, -1), ("col", "row"), scatter_dimension=0, tiled=True
    )
    outer_sums = lax.psum(outer_sums, "expert").astype(f32)

    inner_grad = run_backward(query_rot, key_rot, value_low, mixed_grad, logs, cosine, sine)
    inner_parts = jnp.einsum(
        "td,ctf->cdf", normed, inner_grad, preferred_element_type=f32
    ).astype(bf16)
    inner_parts = split_parts(inner_parts, joined, cuts)
    inner_sums = lax.psum_scatter(
        inner_parts.reshape(col_count * width, -1), ("col", "row"), scatter_dimension=0, tiled=True
    )
    inner_sums = lax.psum(inner_sums, "expert").astype(f32)
    normed_grad = sum(
        jnp.einsum("tf,df->td", inner_grad[c], inner_weight[c], preferred_element_type=f32)
        for c in range(inner_grad.shape[0])
    )
    input_norm_grad, attention_part = norm_back(normed_grad, inputs, first_inverse, attention_full)
    input_gradient = middle_grad + input_norm_grad

    gain_sums = lax.psum(jnp.stack([attention_part, mixture_part]), ("row", "col", "expert"))
    gain_width = attention_gain.shape[0]
    place = lax.axis_index("row") * col_count + lax.axis_index("col")
    gain_sums = lax.dynamic_slice_in_dim(gain_sums, place * gain_width, gain_width, axis=1)
    return (
        layer_output,
        input_gradient,
        inner_sums[:, :query_width],
        inner_sums[:, query_width : query_width + key_width],
        inner_sums[:, query_width + key_width :],
        outer_sums[:, :output_width],
        outer_sums[:, output_width:],
        gain_sums[0],
        gain_sums[1],
        expert_sums[0],
        expert_sums[1],
        expert_sums[2],
    )


def solution(mesh):
    placed = (
        P(("row", "col", "expert"), None),
        P("row", "col"),
        P("row", "col"),
        P("row", "col"),
        P("row", "col"),
        P("row", "col"),
        P(("row", "col")),
        P(("row", "col")),
        P(("row", "col"), "expert", None),
        P(("row", "col"), "expert", None),
        P(("row", "col"), "expert", None),
        P(("row", "col", "expert"), None),
        P(("row", "col", "expert"), None),
    )
    return jax.shard_map(
        shards,
        mesh=mesh,
        in_specs=placed,
        out_specs=(
            P(("row", "col", "expert"), None),
            P(("row", "col", "expert"), None),
            P("row", "col"),
            P("row", "col"),
            P("row", "col"),
            P("row", "col"),
            P("row", "col"),
            P(("row", "col")),
            P(("row", "col")),
            P(("row", "col"), "expert", None),
            P(("row", "col"), "expert", None),
            P(("row", "col"), "expert", None),
        ),
        check_vma=False,
    )
```

```python
import functools

import jax
import jax.numpy as jnp
from jax import lax
from jax.experimental import pallas as pl
from jax.experimental.pallas import tpu as pltpu
from jax.sharding import PartitionSpec as P

HEAD_SIZE = 64
EXPERTS = 32
MOST = 144

score_factor = 0.015625
branch_factor = 0.22
norm_epsilon = 1e-06
rotary_base = 10000.0
masked_score = -1e30
bf16 = jnp.bfloat16
f32 = jnp.float32


def dot(a, b, a_dim, b_dim):
    return lax.dot_general(a, b, (((a_dim,), (b_dim,)), ((), ())), preferred_element_type=f32)


def rotary_tables(sequence_length):
    half_width = HEAD_SIZE // 2
    inverse = rotary_base ** (-(jnp.arange(half_width, dtype=f32) * 2.0 / HEAD_SIZE))
    angles = jnp.arange(sequence_length, dtype=f32)[:, None] * inverse[None, :]
    cosine, sine = jnp.cos(angles), jnp.sin(angles)
    return (
        jnp.concatenate([cosine] * 4, axis=1),
        jnp.concatenate([-sine, sine, -sine, sine], axis=1),
    )


def turned(values):
    half = HEAD_SIZE // 2
    lane = lax.broadcasted_iota(jnp.int32, values.shape, 1)
    ahead = pltpu.roll(values, values.shape[1] - half, 1)
    behind = pltpu.roll(values, half, 1)
    return jnp.where(lane % HEAD_SIZE < half, ahead, behind)


def causal_scores(query, keys, begin):
    scores = dot(query, keys, 1, 1) * score_factor
    rows = begin + lax.broadcasted_iota(jnp.int32, scores.shape, 0)
    return jnp.where(rows >= lax.broadcasted_iota(jnp.int32, scores.shape, 1), scores, masked_score)


def attention_forward(
    query_width, key_width, qkv_ref, cos_ref, sin_ref, query_ref, key_ref, value_ref, mixed_ref, log_ref
):
    length = qkv_ref.shape[1]
    block = min(256, length)
    cosine, sine = cos_ref[...], sin_ref[...]
    for start in range(0, query_width + key_width, 128):
        values = qkv_ref[0, :, start : start + 128]
        rotated = (values * cosine + turned(values) * sine).astype(bf16)
        if start < query_width:
            query_ref[0, :, start : start + 128] = rotated
        else:
            key_ref[0, :, start - query_width : start - query_width + 128] = rotated
    value_ref[0] = qkv_ref[0, :, query_width + key_width :].astype(bf16)
    groups = query_width // key_width
    lane = lax.broadcasted_iota(jnp.int32, (block, 128), 1)
    for begin in range(0, length, block):
        end = begin + block
        logs = jnp.zeros((block, 128), f32)
        for head in range(query_width // HEAD_SIZE):
            here = slice(head * HEAD_SIZE, (head + 1) * HEAD_SIZE)
            shared = slice(head // groups * HEAD_SIZE, (head // groups + 1) * HEAD_SIZE)
            scores = causal_scores(query_ref[0, begin:end, here], key_ref[0, :end, shared], begin)
            row_max = jnp.max(scores, axis=1, keepdims=True)
            weights = jnp.exp(scores - row_max)
            total = jnp.sum(weights, axis=1, keepdims=True)
            probs = (weights * (1.0 / total)).astype(bf16)
            mixed_ref[begin:end, here] = dot(probs, value_ref[0, :end, shared], 1, 0).astype(bf16)
            logs = jnp.where(lane == head, row_max + jnp.log(total), logs)
        log_ref[0, begin:end, :] = logs


def attention_backward(
    query_width,
    key_width,
    query_ref,
    key_ref,
    value_ref,
    grad_ref,
    log_ref,
    cos_ref,
    sin_ref,
    out_ref,
    dq_ref,
    dk_ref,
    dv_ref,
):
    length = query_ref.shape[1]
    block = min(256, length)
    groups = query_width // key_width
    dk_ref[...] = jnp.zeros_like(dk_ref)
    dv_ref[...] = jnp.zeros_like(dv_ref)
    for begin in range(0, length, block):
        end = begin + block
        for head in range(query_width // HEAD_SIZE):
            here = slice(head * HEAD_SIZE, (head + 1) * HEAD_SIZE)
            shared = slice(head // groups * HEAD_SIZE, (head // groups + 1) * HEAD_SIZE)
            query = query_ref[0, begin:end, here]
            keys = key_ref[0, :end, shared]
            grads = grad_ref[begin:end, here]
            scores = causal_scores(query, keys, begin)
            weights = jnp.exp(scores - log_ref[0, begin:end, head : head + 1])
            weight_grad = dot(grads, value_ref[0, :end, shared], 1, 1)
            spread = jnp.sum(weights * weight_grad, axis=1, keepdims=True)
            score_grad = (weights * (weight_grad - spread)).astype(bf16)
            dq_ref[begin:end, here] = dot(score_grad, keys, 1, 0) * score_factor
            dk_ref[:end, shared] += dot(score_grad, query, 0, 0) * score_factor
            dv_ref[:end, shared] += dot(weights.astype(bf16), grads, 0, 0)
    cosine, sine = cos_ref[...], sin_ref[...]
    for start in range(0, query_width + key_width, 128):
        if start < query_width:
            values = dq_ref[:, start : start + 128]
        else:
            values = dk_ref[:, start - query_width : start - query_width + 128]
        out_ref[0, :, start : start + 128] = (values * cosine - turned(values) * sine).astype(bf16)
    out_ref[0, :, query_width + key_width :] = dv_ref[...].astype(bf16)


def params(count):
    return pltpu.CompilerParams(
        dimension_semantics=("arbitrary",) * count, vmem_limit_bytes=56 * 1024 * 1024
    )


def run_forward(qkv, cosine, sine, query_width, key_width):
    parts, length, width = qkv.shape
    whole = lambda c: (c, 0, 0)
    table = pl.BlockSpec((length, 128), lambda c: (0, 0))
    return pl.pallas_call(
        functools.partial(attention_forward, query_width, key_width),
        grid=(parts,),
        in_specs=[pl.BlockSpec((1, length, width), whole), table, table],
        out_specs=[
            pl.BlockSpec((1, length, query_width), whole),
            pl.BlockSpec((1, length, key_width), whole),
            pl.BlockSpec((1, length, key_width), whole),
            pl.BlockSpec((length, query_width), lambda c: (0, c)),
            pl.BlockSpec((1, length, 128), whole),
        ],
        out_shape=[
            jax.ShapeDtypeStruct((parts, length, query_width), bf16),
            jax.ShapeDtypeStruct((parts, length, key_width), bf16),
            jax.ShapeDtypeStruct((parts, length, key_width), bf16),
            jax.ShapeDtypeStruct((length, parts * query_width), bf16),
            jax.ShapeDtypeStruct((parts, length, 128), f32),
        ],
        compiler_params=params(1),
        cost_estimate=pl.CostEstimate(
            flops=4 * length * length * parts * query_width,
            bytes_accessed=8 * parts * length * width,
            transcendentals=parts * length * length * query_width // HEAD_SIZE,
        ),
        name="attention_forward",
    )(qkv, cosine, sine)


def run_backward(query, key, value, grad, logs, cosine, sine):
    parts, length, query_width = query.shape
    key_width = key.shape[2]
    width = query_width + 2 * key_width
    whole = lambda c: (c, 0, 0)
    table = pl.BlockSpec((length, 128), lambda c: (0, 0))
    return pl.pallas_call(
        functools.partial(attention_backward, query_width, key_width),
        grid=(parts,),
        in_specs=[
            pl.BlockSpec((1, length, query_width), whole),
            pl.BlockSpec((1, length, key_width), whole),
            pl.BlockSpec((1, length, key_width), whole),
            pl.BlockSpec((length, query_width), lambda c: (0, c)),
            pl.BlockSpec((1, length, 128), whole),
            table,
            table,
        ],
        out_specs=pl.BlockSpec((1, length, width), whole),
        out_shape=jax.ShapeDtypeStruct((parts, length, width), bf16),
        scratch_shapes=[
            pltpu.VMEM((length, query_width), f32),
            pltpu.VMEM((length, key_width), f32),
            pltpu.VMEM((length, key_width), f32),
        ],
        compiler_params=params(1),
        cost_estimate=pl.CostEstimate(
            flops=10 * length * length * parts * query_width,
            bytes_accessed=6 * parts * length * width,
            transcendentals=parts * length * length * query_width // HEAD_SIZE,
        ),
        name="attention_backward",
    )(query, key, value, grad, logs, cosine, sine)


def dispatch_kernel(slot_ref, gate_ref, second_ref, grad_ref, rows_ref, grads_ref, gates_ref):
    expert = pl.program_id(1)
    slots = slot_ref[0, pl.ds(expert, 1), :]
    gates = gate_ref[0, pl.ds(expert, 1), :]
    match = lax.broadcasted_iota(jnp.int32, (MOST, slots.shape[1]), 0) == slots
    picks = match.astype(f32).astype(bf16)
    rows_ref[0, 0] = dot(picks, second_ref[0], 1, 0).astype(bf16)
    grads_ref[0, 0] = dot(picks, grad_ref[0], 1, 0).astype(bf16)
    gate_column = jnp.sum(jnp.where(match, gates, 0.0), axis=1, keepdims=True)
    gates_ref[0, 0] = jnp.broadcast_to(gate_column, (MOST, 128))


def run_dispatch(slots, gates, second, grad):
    sources, experts, length = slots.shape
    width = second.shape[2]
    table = pl.BlockSpec((1, experts, length), lambda s, e: (s, 0, 0))
    rows = pl.BlockSpec((1, length, width), lambda s, e: (s, 0, 0))
    out = lambda n: pl.BlockSpec((1, 1, MOST, n), lambda s, e: (e, s, 0, 0))
    return pl.pallas_call(
        dispatch_kernel,
        grid=(sources, experts),
        in_specs=[table, table, rows, rows],
        out_specs=[out(width), out(width), out(128)],
        out_shape=[
            jax.ShapeDtypeStruct((experts, sources, MOST, width), bf16),
            jax.ShapeDtypeStruct((experts, sources, MOST, width), bf16),
            jax.ShapeDtypeStruct((experts, sources, MOST, 128), f32),
        ],
        compiler_params=params(2),
        cost_estimate=pl.CostEstimate(
            flops=4 * sources * experts * MOST * length * width,
            bytes_accessed=4 * sources * experts * MOST * width,
            transcendentals=0,
        ),
        name="dispatch",
    )(slots, gates, second, grad)


def expert_kernel(rows_ref, grads_ref, gates_ref, weight_ref, out_ref, back_ref, gate_grad_ref, weight_grad_ref):
    sources, slots, width = rows_ref.shape[1:]
    count = sources * slots
    pieces, _, _, part, hidden = weight_ref.shape
    rows = rows_ref[0].reshape(count, width)
    grads = grads_ref[0].reshape(count, width)
    gates = gates_ref[0].reshape(count, 128)[:, :1] * branch_factor
    gate_weight = weight_ref[:, 0, 0].reshape(width, hidden)
    up_weight = weight_ref[:, 1, 0].reshape(width, hidden)
    down_weight = weight_ref[:, 2, 0].reshape(width, hidden)
    gate_pre = dot(rows, gate_weight, 1, 0)
    up_pre = dot(rows, up_weight, 1, 0)
    sigmoid = 1.0 / (1.0 + jnp.exp(-gate_pre))
    silu = gate_pre * sigmoid
    act = (silu * up_pre).astype(bf16).astype(f32)
    act_raw = dot(grads, down_weight, 1, 0)
    gate_grad = jnp.sum(act * act_raw, axis=1, keepdims=True) * branch_factor
    gate_grad_ref[0] = jnp.broadcast_to(gate_grad, (count, 128)).reshape(sources, slots, 128)
    scaled = (gates * act).astype(bf16)
    act_grad = gates * act_raw
    gate_low = (act_grad * up_pre * sigmoid * (1.0 + gate_pre * (1.0 - sigmoid))).astype(bf16)
    up_low = (act_grad * silu).astype(bf16)
    back = dot(gate_low, gate_weight, 1, 1) + dot(up_low, up_weight, 1, 1)
    back_ref[0] = back.astype(bf16).reshape(sources, slots, width)
    out_ref[0] = dot(scaled, down_weight, 1, 1).astype(bf16).reshape(sources, slots, width)
    shape = (pieces, part, hidden)
    weight_grad_ref[:, 0, 0] = dot(rows, gate_low, 0, 0).astype(bf16).reshape(shape)
    weight_grad_ref[:, 1, 0] = dot(rows, up_low, 0, 0).astype(bf16).reshape(shape)
    weight_grad_ref[:, 2, 0] = dot(grads, scaled, 0, 0).astype(bf16).reshape(shape)


def run_experts(rows, grads, gates, weights):
    experts, sources, slots, width = rows.shape
    pieces, kinds, _, part, hidden = weights.shape
    row = lambda n: pl.BlockSpec((1, sources, slots, n), lambda e: (e, 0, 0, 0))
    weight = pl.BlockSpec((pieces, kinds, 1, part, hidden), lambda e: (0, 0, e, 0, 0))
    return pl.pallas_call(
        expert_kernel,
        grid=(experts,),
        in_specs=[row(width), row(width), row(128), weight],
        out_specs=[row(width), row(width), row(128), weight],
        out_shape=[
            jax.ShapeDtypeStruct(rows.shape, bf16),
            jax.ShapeDtypeStruct(rows.shape, bf16),
            jax.ShapeDtypeStruct(gates.shape, f32),
            jax.ShapeDtypeStruct(weights.shape, bf16),
        ],
        compiler_params=params(1),
        cost_estimate=pl.CostEstimate(
            flops=18 * experts * sources * slots * width * hidden,
            bytes_accessed=8 * experts * sources * slots * width + 4 * weights.size,
            transcendentals=experts * sources * slots * hidden,
        ),
        name="experts",
    )(rows, grads, gates, weights)


def combine_kernel(slot_ref, rows_ref, out_ref, picks_ref):
    experts, length = slot_ref.shape[1:]
    for expert in range(experts):
        match = lax.broadcasted_iota(jnp.int32, (MOST, length), 0) == slot_ref[0, expert : expert + 1, :]
        picks_ref[expert * MOST : (expert + 1) * MOST, :] = match.astype(f32).astype(bf16)
    rows = rows_ref[:, 0].reshape(experts * MOST, rows_ref.shape[3])
    out_ref[0] = dot(picks_ref[...], rows, 0, 0).astype(bf16)


def combine_gates_kernel(slot_ref, rows_ref, gate_ref, out_ref, gate_out_ref, picks_ref):
    combine_kernel(slot_ref, rows_ref, out_ref, picks_ref)
    experts, length = slot_ref.shape[1:]
    for expert in range(experts):
        match = lax.broadcasted_iota(jnp.int32, (MOST, length), 0) == slot_ref[0, expert : expert + 1, :]
        column = gate_ref[expert, 0][:, :1]
        gate_out_ref[0, expert : expert + 1, :] = jnp.sum(
            jnp.where(match, column, 0.0), axis=0, keepdims=True
        )


def run_combine(slots, rows, gate_grads=None):
    sources, experts, length = slots.shape
    width = rows.shape[3]
    table = pl.BlockSpec((1, experts, length), lambda s: (s, 0, 0))
    row = lambda n: pl.BlockSpec((experts, 1, MOST, n), lambda s: (0, s, 0, 0))
    out_spec = pl.BlockSpec((1, length, width), lambda s: (s, 0, 0))
    out_shape = jax.ShapeDtypeStruct((sources, length, width), bf16)
    common = dict(
        grid=(sources,),
        scratch_shapes=[pltpu.VMEM((experts * MOST, length), bf16)],
        compiler_params=params(1),
        cost_estimate=pl.CostEstimate(
            flops=2 * sources * experts * MOST * length * width,
            bytes_accessed=2 * rows.size + 2 * sources * length * width,
            transcendentals=0,
        ),
    )
    if gate_grads is None:
        return pl.pallas_call(
            combine_kernel,
            in_specs=[table, row(width)],
            out_specs=out_spec,
            out_shape=out_shape,
            name="combine",
            **common,
        )(slots, rows)
    return pl.pallas_call(
        combine_gates_kernel,
        in_specs=[table, row(width), row(128)],
        out_specs=[out_spec, table],
        out_shape=[out_shape, jax.ShapeDtypeStruct(slots.shape, f32)],
        name="combine_gates",
        **common,
    )(slots, rows, gate_grads)


def inverse_norm(values):
    return lax.rsqrt(jnp.mean(values * values, axis=-1, keepdims=True) + norm_epsilon)


def norm_back(incoming, values, inverse, gain_row):
    scaled = incoming * gain_row
    mean = jnp.mean(scaled * values, axis=-1, keepdims=True)
    grad = inverse * scaled - values * (inverse * inverse * inverse * mean)
    return grad, jnp.sum(incoming * values * inverse, axis=0)


def join_parts(parts, joined, cuts):
    if joined == 1:
        return parts
    count, width, _ = parts.shape
    pieces = jnp.split(parts, cuts, axis=2)
    return jnp.concatenate(
        [
            piece.reshape(count // joined, joined, width, -1)
            .transpose(0, 2, 1, 3)
            .reshape(count // joined, width, -1)
            for piece in pieces
        ],
        axis=2,
    )


def split_parts(parts, joined, cuts):
    if joined == 1:
        return parts
    count, width, _ = parts.shape
    pieces = jnp.split(parts, [cut * joined for cut in cuts], axis=2)
    return jnp.concatenate(
        [
            piece.reshape(count, width, joined, -1)
            .transpose(0, 2, 1, 3)
            .reshape(count * joined, width, -1)
            for piece in pieces
        ],
        axis=2,
    )


def shifted(values, shift, count):
    return lax.ppermute(values, "expert", [(i, (i + shift) % count) for i in range(count)])


def gather_steps(values, count):
    me = lax.axis_index("expert")
    whole = jnp.zeros((count,) + values.shape, values.dtype)
    for shift in range(count):
        piece = shifted(values, shift, count) if shift else values
        whole = lax.dynamic_update_index_in_dim(whole, piece, (me - shift + count) % count, 0)
    return whole


def sum_steps(values, count):
    me = lax.axis_index("expert")
    total = None
    for shift in range(count):
        piece = lax.dynamic_index_in_dim(values, (me + shift) % count, axis=0, keepdims=False)
        piece = (shifted(piece, shift, count) if shift else piece).astype(f32)
        total = piece if total is None else total + piece
    return total


def shards(
    tokens,
    query_weight,
    key_projection,
    value_projection,
    output_weight,
    router_weight,
    attention_gain,
    mixture_gain,
    gate_weight,
    up_weight,
    down_weight,
    choices,
    cotangent,
):
    col_count, row_count, sources = (lax.axis_size(name) for name in ("col", "row", "expert"))
    length, width = tokens.shape
    query_width, key_width, output_width = (
        query_weight.shape[1],
        key_projection.shape[1],
        output_weight.shape[1],
    )
    router_width = router_weight.shape[1]
    local_experts = gate_weight.shape[1]
    inner = query_width + 2 * key_width

    gains = lax.all_gather(jnp.stack([attention_gain, mixture_gain]), ("row", "col"), axis=1, tiled=True)
    packed = jnp.concatenate(
        [query_weight, key_projection, value_projection, output_weight, router_weight], axis=1
    )
    packed = lax.all_gather(packed, ("col", "row"), axis=0, tiled=True)
    packed = packed.reshape(col_count, width, packed.shape[1])
    joined = max(1, 128 // key_width)
    cuts = (query_width, query_width + key_width)
    inner_weight = join_parts(packed[:, :, :inner], joined, cuts)
    outer_weight = packed[:, :, inner : inner + output_width]
    router_parts = packed[:, :, inner + output_width :]
    router_full = router_parts.transpose(1, 0, 2).reshape(width, EXPERTS)

    choices_all = lax.all_gather(choices, "expert", axis=0)
    cotangent_all = gather_steps(cotangent, sources)
    weights = jnp.stack([gate_weight, up_weight, down_weight]).transpose(0, 2, 1, 3)
    weights_all = lax.all_gather(weights, ("row", "col"), axis=0)

    expert_ids = jnp.arange(EXPERTS, dtype=jnp.int32)
    chosen = jnp.any(
        choices_all.transpose(0, 2, 1)[:, :, None, :] == expert_ids[None, None, :, None], axis=1
    )
    earlier = (jnp.arange(length)[:, None] < jnp.arange(length)[None, :]).astype(bf16)
    ranks = jnp.einsum("set,tu->seu", chosen.astype(bf16), earlier, preferred_element_type=f32)
    slots_all = jnp.where(chosen, ranks.astype(jnp.int32), -1)
    source = lax.axis_index("expert")
    slots = lax.dynamic_slice_in_dim(slots_all, source * local_experts, local_experts, axis=1)

    cosine, sine = rotary_tables(length)
    attention_full, mixture_full = gains[0].astype(f32), gains[1].astype(f32)
    inputs = tokens.astype(f32)
    first_inverse = inverse_norm(inputs)
    normed = (attention_full * inputs * first_inverse).astype(bf16)
    qkv = jnp.einsum("td,cdf->ctf", normed, inner_weight, preferred_element_type=f32)
    query_rot, key_rot, value_low, mixed, logs = run_forward(
        qkv, cosine, sine, query_width * joined, key_width * joined
    )
    branch = jnp.concatenate(
        [jnp.dot(mixed, outer_weight[c], preferred_element_type=f32) for c in range(col_count)], axis=1
    )
    middle = inputs + branch_factor * branch
    second_inverse = inverse_norm(middle)
    second = (mixture_full * middle * second_inverse).astype(bf16)

    second, weights_all = lax.optimization_barrier((second, weights_all))
    second_all = lax.all_gather(second, "expert", axis=0)
    logits = jnp.einsum("de,std->set", router_full, second_all, preferred_element_type=f32)
    top = jnp.max(jnp.where(chosen, logits, masked_score), axis=1, keepdims=True)
    exped = jnp.where(chosen, jnp.exp(jnp.where(chosen, logits - top, 0.0)), 0.0)
    gates_all = exped / jnp.sum(exped, axis=1, keepdims=True)
    gates = lax.dynamic_slice_in_dim(gates_all, source * local_experts, local_experts, axis=1)
    own_gates = lax.dynamic_index_in_dim(gates_all, source, axis=0, keepdims=False)

    rows, grads, slot_gates = run_dispatch(slots, gates, second_all, cotangent_all)
    outs, backs, slot_gate_grads, weight_grads = run_experts(rows, grads, slot_gates, weights_all)
    back_sums, gate_grads = run_combine(slots, backs, slot_gate_grads)
    gate_grads = lax.all_to_all(gate_grads, "expert", split_axis=0, concat_axis=0).reshape(EXPERTS, length)
    second_grad = sum_steps(back_sums, sources)
    out_sums = run_combine(slots, outs)
    combined = sum_steps(out_sums, sources)
    layer_output = (middle + combined).astype(bf16)
    expert_sums = lax.psum_scatter(weight_grads, ("row", "col"), scatter_dimension=0)

    mean_grad = jnp.sum(own_gates * gate_grads, axis=0, keepdims=True)
    logit_grad = (own_gates * (gate_grads - mean_grad)).astype(bf16)
    router_part = jnp.einsum("td,et->de", second, logit_grad, preferred_element_type=f32)
    second_grad = second_grad + jnp.einsum(
        "et,de->td", logit_grad, router_full, preferred_element_type=f32
    )
    middle_norm_grad, mixture_part = norm_back(second_grad, middle, second_inverse, mixture_full)
    middle_grad = cotangent.astype(f32) + middle_norm_grad
    branch_grad = (branch_factor * middle_grad).astype(bf16)
    branch_parts = [
        branch_grad[:, c * output_width : (c + 1) * output_width] for c in range(col_count)
    ]
    mixed_grad = sum(
        jnp.einsum("td,fd->tf", branch_parts[c], outer_weight[c], preferred_element_type=f32)
        for c in range(col_count)
    ).astype(bf16)
    output_parts = jnp.stack(
        [
            jnp.concatenate(
                [
                    jnp.einsum("tf,td->fd", mixed, branch_parts[c], preferred_element_type=f32),
                    router_part[:, c * router_width : (c + 1) * router_width],
                ],
                axis=1,
            ).astype(bf16)
            for c in range(col_count)
        ]
    )
    output_parts, expert_sums = lax.optimization_barrier((output_parts, expert_sums))
    outer_sums = lax.psum_scatter(
        output_parts.reshape(col_count * width, -1), ("col", "row"), scatter_dimension=0, tiled=True
    )
    outer_sums = lax.psum(outer_sums, "expert").astype(f32)

    inner_grad = run_backward(query_rot, key_rot, value_low, mixed_grad, logs, cosine, sine)
    inner_parts = jnp.einsum(
        "td,ctf->cdf", normed, inner_grad, preferred_element_type=f32
    ).astype(bf16)
    inner_parts = split_parts(inner_parts, joined, cuts)
    inner_sums = lax.psum_scatter(
        inner_parts.reshape(col_count * width, -1), ("col", "row"), scatter_dimension=0, tiled=True
    )
    inner_sums = lax.psum(inner_sums, "expert").astype(f32)
    normed_grad = sum(
        jnp.einsum("tf,df->td", inner_grad[c], inner_weight[c], preferred_element_type=f32)
        for c in range(inner_grad.shape[0])
    )
    input_norm_grad, attention_part = norm_back(normed_grad, inputs, first_inverse, attention_full)
    input_gradient = middle_grad + input_norm_grad

    gain_sums = lax.psum(jnp.stack([attention_part, mixture_part]), ("row", "col", "expert"))
    expert_sums = expert_sums.transpose(0, 2, 1, 3).astype(f32)
    gain_width = attention_gain.shape[0]
    place = lax.axis_index("row") * col_count + lax.axis_index("col")
    gain_sums = lax.dynamic_slice_in_dim(gain_sums, place * gain_width, gain_width, axis=1)
    return (
        layer_output,
        input_gradient,
        inner_sums[:, :query_width],
        inner_sums[:, query_width : query_width + key_width],
        inner_sums[:, query_width + key_width :],
        outer_sums[:, :output_width],
        outer_sums[:, output_width:],
        gain_sums[0],
        gain_sums[1],
        expert_sums[0],
        expert_sums[1],
        expert_sums[2],
    )


def solution(mesh):
    placed = (
        P(("row", "col", "expert"), None),
        P("row", "col"),
        P("row", "col"),
        P("row", "col"),
        P("row", "col"),
        P("row", "col"),
        P(("row", "col")),
        P(("row", "col")),
        P(("row", "col"), "expert", None),
        P(("row", "col"), "expert", None),
        P(("row", "col"), "expert", None),
        P(("row", "col", "expert"), None),
        P(("row", "col", "expert"), None),
    )
    return jax.shard_map(
        shards,
        mesh=mesh,
        in_specs=placed,
        out_specs=(
            P(("row", "col", "expert"), None),
            P(("row", "col", "expert"), None),
            P("row", "col"),
            P("row", "col"),
            P("row", "col"),
            P("row", "col"),
            P("row", "col"),
            P(("row", "col")),
            P(("row", "col")),
            P(("row", "col"), "expert", None),
            P(("row", "col"), "expert", None),
            P(("row", "col"), "expert", None),
        ),
        check_vma=False,
    )
```
